32 devices in a mesh: dp: 8 (over y, x, core), mp: 4 (over z).
Axes of the slice: x: 2, y: 2, z: 4, core: 2. Of those that a mesh axis runs over, the one named last changes fastest.
Arguments:
- hidden_acts: bfloat16 [12288, 1024], P('dp'), may hold values from -3072 to 3072
- out_grads: bfloat16 [12288, 8192], P('dp', 'mp'), may hold values from -6 to 6
- token_counts: int32 [8], P('dp'), may hold values from 1 to 1536, as said below
- down_weight: bfloat16 [1024, 8192], P(None, 'mp'), may hold values from -0.0625 to 0.0625
- owner_map: int32 [8], replicated, may hold values from 0 to 7, each once
- master: float32 [1024, 8192], P('dp', 'mp'), may hold values from -0.046875 to 0.046875
- moment1: float32 [1024, 8192], P('dp', 'mp'), may hold values from -6 to 6
- moment2: bfloat16 [1024, 8192], P('dp', 'mp'), may hold values from 0.099609375 to 10
Outputs:
- master_new: float32 [1024, 8192], P('dp', 'mp')
- moment1_new: float32 [1024, 8192], P('dp', 'mp')
- moment2_new: bfloat16 [1024, 8192], P('dp', 'mp')
- weights_new: bfloat16 [1024, 8192], P(None, 'mp')
- input_grads: bfloat16 [12288, 1024], P('dp', 'mp')
The draws below stay inside these ranges and needn't reach their ends.
Inputs may be any that keep to these rules, and one draw needn't show every extreme that they name: `token_counts`: the last worker is always full; the others hold from about a third to all of their 1536 slots, rising along the workers.
All inputs are finite; a program needn't handle non-finite values.
Results may differ from the reference program's by a relative error of at most 0.0026.
Values may be sent and summed in bfloat16 or wider, within the bound.
A program may use at most 128 MiB of HBM per device.

```python
import math
import jax
import jax.numpy as jnp
from jax import lax

D = 8192
TOK_DEV = 1536
HB = 1024
TOKENS = 12288
N_DP = 8


def draw_token_counts(key, part):
    workers = jnp.arange(N_DP, dtype=jnp.int32)
    lowest = TOK_DEV // 3
    base = lowest + workers * (TOK_DEV - lowest) // max(N_DP - 1, 1)
    jitter = jax.random.randint(jax.random.fold_in(key, 17), (N_DP,), 0, TOK_DEV // 8 + 1)
    counts = jnp.maximum(base - jitter, 1)
    return jnp.where(workers == N_DP - 1, TOK_DEV, counts).astype(jnp.int32)


def spiked(array, stream_key, source, target, parts, factor):
    owner, partner = [(jnp.arange(array.shape[position]) // (array.shape[position] // parts)).reshape([-1 if axis == position else 1 for axis in range(array.ndim)]) for position in (source, target)]
    chosen = jax.random.permutation(stream_key, parts)[partner]
    strong = (owner == chosen) | (owner == (partner + parts // 2) % parts)
    return jnp.where(strong, factor * array, array)


def levels(own_key, extent, pieces, least, high):
    gain = 1.0
    for position, shards_of in pieces:
        steps = jax.random.uniform(jax.random.fold_in(jax.random.fold_in(own_key, 6), position), (shards_of,), jnp.float32, least / len(pieces), high / len(pieces))
        gain = gain * jnp.repeat(jnp.exp(steps), extent[position] // shards_of).reshape((-1,) + (1,) * (len(extent) - 1 - position))
    return gain


def scatter_about(own_key, dims, width, limit, pieces=(), kind=jnp.bfloat16):
    result = width * jax.random.normal(own_key, dims, jnp.float32)
    if pieces:
        result = result * levels(own_key, dims, pieces, -0.22, 0.18)
    return jnp.clip(result, -limit, limit).astype(kind)


def bell_draw_with(key, extent, deviation, limit, pieces, heavy, kind=jnp.bfloat16):
    result = deviation * jax.random.normal(key, extent, jnp.float32)
    if pieces:
        result = result * levels(key, extent, pieces, -0.22, 0.18)
    return jnp.clip(spiked(result, jax.random.fold_in(key, 3), *heavy), -limit, limit).astype(kind)


def setup_inputs(seed: int = 0) -> dict:
    key_of = jax.random.split(jax.random.key(seed), 9)
    return {
        "hidden_acts": bell_draw_with(key_of[0], (TOKENS, HB), (N_DP + TOK_DEV // 4), 3072.0, ((0, 8),), (0, 1, 8, 2.0)),
        "out_grads": scatter_about(key_of[1], (TOKENS, D), 1.0, 6.0, ((0, 8), (1, 4))),
        "token_counts": draw_token_counts(jax.random.fold_in(key_of[8], 71), 0),
        "down_weight": scatter_about(key_of[3], (HB, D), D ** -0.5, 0.0625, ((1, 4),)),
        "owner_map": jax.random.permutation(key_of[4], N_DP).astype(jnp.int32),
        "master": scatter_about(key_of[5], (HB, D), 0.003, 0.046875, ((0, 8), (1, 4)), jnp.float32),
        "moment1": scatter_about(key_of[6], (HB, D), 1.0, 6.0, ((0, 8), (1, 4)), jnp.float32),
        "moment2": jnp.clip(jnp.exp(math.log(10.0) - 4.609084 * jax.random.uniform(key_of[7], (HB, D), jnp.float32) ** levels(key_of[7], (HB, D), ((0, 8), (1, 4)), -0.2, 0.2)), 0.099609375, 10.0).astype(jnp.bfloat16),
    }


beta_one = 0.9
beta_two = 0.95
learn_rate = 0.0003
epsilon = 1e-08
correct_one = 1.0 - 0.9 ** 50
correct_two = 1.0 - 0.95 ** 50

def reference(hidden_acts, out_grads, token_counts, down_weight, owner_map, master, moment1, moment2):
    block = HB // N_DP
    positions = jnp.arange(TOKENS, dtype=jnp.int32)
    worker_of = positions // TOK_DEV
    valid = positions % TOK_DEV < token_counts[worker_of]
    masked = jnp.where(valid[:, None], out_grads, jnp.zeros_like(out_grads))

    def accumulate(total_sum, worker):
        start = (worker * TOK_DEV).astype(jnp.int32)
        acts = lax.dynamic_slice_in_dim(hidden_acts, start, TOK_DEV, 0)
        grads = lax.dynamic_slice_in_dim(masked, start, TOK_DEV, 0)
        term = lax.dot_general(acts, grads, (((0,), (0,)), ((), ())), preferred_element_type=jnp.float32)
        term = lax.optimization_barrier(term.astype(jnp.bfloat16)).astype(jnp.float32)
        return (total_sum + term, None)
    summed, _ = lax.scan(accumulate, jnp.zeros((HB, D), jnp.float32), jnp.arange(N_DP, dtype=jnp.int32))
    total = jnp.sum(token_counts).astype(jnp.float32)
    grad = summed / total
    grad_slots = jnp.take(grad.reshape(N_DP, block, D), owner_map, axis=0).reshape(HB, D)
    moment1_new = beta_one * moment1 + (1.0 - beta_one) * grad_slots
    second = beta_two * moment2.astype(jnp.float32) + (1.0 - beta_two) * grad_slots * grad_slots
    moment2_new = second.astype(jnp.bfloat16)
    master_new = master - learn_rate * (moment1_new / correct_one) / (jnp.sqrt(second / correct_two) + epsilon)
    slot_weights = master_new.astype(jnp.bfloat16).reshape(N_DP, block, D)
    weights_new = jnp.zeros((N_DP, block, D), jnp.bfloat16).at[owner_map].set(slot_weights).reshape(HB, D)
    input_grads = lax.dot_general(masked, down_weight, (((1,), (1,)), ((), ())), preferred_element_type=jnp.float32).astype(jnp.bfloat16)
    return (master_new, moment1_new, moment2_new, weights_new, input_grads)
```

```python
import functools

import jax
import jax.numpy as jnp
from jax import lax
from jax.experimental import pallas as pl
from jax.experimental.pallas import tpu as pltpu
from jax.sharding import PartitionSpec as P

beta_one = 0.9
beta_two = 0.95
learn_rate = 0.0003
epsilon = 1e-08
correct_one = 1.0 - 0.9**50
correct_two = 1.0 - 0.95**50

MESH = pl.DeviceIdType.MESH
F32 = jnp.float32
BF16 = jnp.bfloat16
ROW_CHUNKS = 4
COL_CHUNKS = 4


def kernel(
    chips, depth,
    acts_hbm, grads_hbm, count_smem, weight_hbm, owner_smem, master_hbm, moment1_hbm, moment2_hbm,
    master_out, moment1_out, moment2_out, weights_out, input_out,
    acts, acts_t, grads, weight, master, moment1, moment2,
    pick, part, from_mate, to_chip, from_chip, own_sum,
    gathered, z_send, z_recv, z_own, z_out,
    count_tile, count_mate, count_pair, count_chip,
    load_sem, grads_sem, out_sem,
    mate_send, mate_recv, chip_send, chip_recv,
    spread_send, spread_recv, relay_send, relay_recv,
    zs_sem, zr_sem, count_send, count_recv,
):
    rows, columns = grads.shape
    hidden = acts.shape[1]
    slots = 2 * chips
    block = hidden // slots
    share = hidden // depth
    rc = rows // ROW_CHUNKS
    cc = columns // COL_CHUNKS
    tile = 256

    me = lax.axis_index("dp")
    z = lax.axis_index("mp")
    core = lax.rem(me, 2)
    chip = me // 2
    mate = me + 1 - 2 * core
    mate_id = (mate, z)

    def chip_id(k):
        return (2 * lax.rem(chip + k, chips) + core, z)

    def z_id(k):
        return (me, lax.rem(z + k, depth))

    def grads_copy(r):
        span = pl.ds(pl.multiple_of(r * rc, rc), rc)
        return pltpu.make_async_copy(grads_hbm.at[span], grads.at[span], grads_sem.at[r])

    for r in range(ROW_CHUNKS):
        grads_copy(r).start()
    loads = [
        pltpu.make_async_copy(source, target, load_sem.at[i])
        for i, (source, target) in enumerate(
            [
                (weight_hbm, weight),
                (acts_hbm, acts),
                (master_hbm, master),
                (moment1_hbm, moment1),
                (moment2_hbm, moment2),
            ]
        )
    ]
    for copy in loads:
        copy.start()

    barrier = pltpu.get_barrier_semaphore()
    pl.semaphore_signal(barrier, inc=1, device_id=mate_id, device_id_type=MESH)

    @pl.loop(1, chips)
    def _(k):
        pl.semaphore_signal(barrier, inc=1, device_id=chip_id(k), device_id_type=MESH)

    for k in range(1, depth):
        pl.semaphore_signal(barrier, inc=1, device_id=z_id(k), device_id_type=MESH)
    pl.semaphore_wait(barrier, 1 + (chips - 1) + (depth - 1))

    count = count_smem[0]
    count_tile[...] = jnp.full(count_tile.shape, count, jnp.int32)

    def count_mate_copy():
        return pltpu.make_async_remote_copy(
            count_tile, count_mate, count_send.at[0], count_recv.at[0], mate_id, MESH
        )

    def count_chip_copy(k):
        return pltpu.make_async_remote_copy(
            count_pair, count_chip.at[k], count_send.at[k], count_recv.at[k], chip_id(k), MESH
        )

    count_mate_copy().start()

    def feature(r, target):
        span = pl.ds(pl.multiple_of(r * rc, rc), rc)
        value = lax.dot_general(
            grads[span, :],
            weight[pl.ds(pl.multiple_of(target * share, share), share), :],
            (((1,), (1,)), ((), ())),
            preferred_element_type=F32,
        )
        position = lax.broadcasted_iota(jnp.int32, value.shape, 0) + r * rc
        return span, jnp.where(position < count, value, 0.0)

    def z_copy(k, r):
        span = pl.ds(pl.multiple_of(r * rc, rc), rc)
        return pltpu.make_async_remote_copy(
            z_send.at[k - 1, span], z_recv.at[k - 1, span],
            zs_sem.at[k - 1, r], zr_sem.at[k - 1, r], z_id(k), MESH,
        )

    def feature_block(k, first):
        @pl.loop(0, ROW_CHUNKS)
        def _(r):
            if first:
                grads_copy(r).wait()
            span, value = feature(r, lax.rem(z + k, depth))
            z_send[k - 1, span, :] = value.astype(BF16)
            z_copy(k, r).start()

    order = [(depth // 2 + i) % depth for i in range(depth)]
    order = [k for k in order if k]
    loads[0].wait()
    feature_block(order[0], True)

    count_mate_copy().wait_recv()
    count_pair[...] = count_tile[...] + count_mate[...]

    @pl.loop(1, chips)
    def _(k):
        count_chip_copy(k).start()

    loads[1].wait()

    @pl.loop(0, slots)
    def _(j):
        span = pl.ds(pl.multiple_of(j * block, block), block)
        first = owner_smem[j] * block
        unit = lax.broadcasted_iota(jnp.int32, (block, hidden), 1)
        row = lax.broadcasted_iota(jnp.int32, (block, hidden), 0)
        pick[span, :] = jnp.where(unit == row + first, 1.0, 0.0).astype(BF16)

    @pl.loop(0, hidden // tile)
    def _(i):
        span = pl.ds(pl.multiple_of(i * tile, tile), tile)
        turned = lax.dot_general(
            pick[span, :], acts[...], (((1,), (1,)), ((), ())), preferred_element_type=F32
        )
        position = lax.broadcasted_iota(jnp.int32, turned.shape, 1)
        acts_t[span, :] = jnp.where(position < count, turned, 0.0).astype(BF16)

    def mate_copy(q):
        return pltpu.make_async_remote_copy(
            part.at[q, :, 1 - core], from_mate.at[q], mate_send.at[q], mate_recv.at[q],
            mate_id, MESH,
        )

    def chip_copy(q, k):
        return pltpu.make_async_remote_copy(
            to_chip.at[q, k], from_chip.at[q, k], chip_send.at[q, k], chip_recv.at[q, k],
            chip_id(k), MESH,
        )

    pairs = tile // (2 * block)

    def partial_chunk(q):
        across = pl.ds(pl.multiple_of(q * cc, cc), cc)

        @pl.loop(0, hidden // tile)
        def _(i):
            span = pl.ds(pl.multiple_of(i * tile, tile), tile)
            value = jnp.dot(acts_t[span, :], grads[:, across], preferred_element_type=F32)
            part[q, pl.ds(i * pairs, pairs)] = value.astype(BF16).reshape(pairs, 2, block, cc)

        mate_copy(q).start()

    def pair_chunk(q):
        mate_copy(q).wait_recv()

        @pl.loop(1, chips)
        def _(k):
            there = lax.rem(chip + k, chips)
            both = part[q, there, core].astype(F32) + from_mate[q, there].astype(F32)
            to_chip[q, k] = both.astype(BF16)
            chip_copy(q, k).start()

        own_sum[q] = part[q, chip, core].astype(F32) + from_mate[q, chip].astype(F32)

    partial_chunk(0)

    @pl.loop(1, COL_CHUNKS)
    def _(q):
        partial_chunk(q)
        pair_chunk(q - 1)

    pair_chunk(COL_CHUNKS - 1)

    for k in order[1:]:
        feature_block(k, False)

    @pl.loop(0, ROW_CHUNKS)
    def _(r):
        span, value = feature(r, z)
        z_own[span, :] = value

    @pl.loop(1, chips)
    def _(k):
        count_chip_copy(k).wait_recv()

    total = lax.fori_loop(1, chips, lambda k, t: t + count_chip[k], count_pair[...])
    total = total[0:1, 0:1].astype(F32)
    for copy in loads[2:]:
        copy.wait()

    def spread_copy(q, k):
        across = pl.ds(pl.multiple_of(q * cc, cc), cc)
        return pltpu.make_async_remote_copy(
            gathered.at[me, :, across], gathered.at[me, :, across],
            spread_send.at[q, k], spread_recv.at[q, k], chip_id(k), MESH,
        )

    def relay_copy(q, k):
        slot = 2 * lax.rem(chip + chips - k, chips) + core
        across = pl.ds(pl.multiple_of(q * cc, cc), cc)
        return pltpu.make_async_remote_copy(
            gathered.at[slot, :, across], gathered.at[slot, :, across],
            relay_send.at[q, k], relay_recv.at[q, k], mate_id, MESH,
        )

    @pl.loop(0, COL_CHUNKS)
    def _(q):
        across = pl.ds(pl.multiple_of(q * cc, cc), cc)

        @pl.loop(1, chips)
        def _(k):
            chip_copy(q, k).wait_recv()
            own_sum[q] = own_sum[q] + from_chip[q, k].astype(F32)

        grad = own_sum[q] / total
        moment1_new = beta_one * moment1[:, across] + (1.0 - beta_one) * grad
        second = beta_two * moment2[:, across].astype(F32) + (1.0 - beta_two) * grad * grad
        moment1[:, across] = moment1_new
        moment2[:, across] = second.astype(BF16)
        master_new = master[:, across] - learn_rate * (moment1_new / correct_one) / (
            jnp.sqrt(second / correct_two) + epsilon
        )
        master[:, across] = master_new
        gathered[me, :, across] = master_new.astype(BF16)

        @pl.loop(1, chips)
        def _(k):
            spread_copy(q, k).start()

        relay_copy(q, 0).start()

    stores = [
        pltpu.make_async_copy(source, target, out_sem.at[i])
        for i, (source, target) in enumerate(
            [
                (master, master_out),
                (moment1, moment1_out),
                (moment2, moment2_out),
                (gathered, weights_out),
                (z_out, input_out),
            ]
        )
    ]
    for copy in stores[:3]:
        copy.start()

    @pl.loop(0, COL_CHUNKS)
    def _(q):
        @pl.loop(1, chips)
        def _(k):
            spread_copy(q, k).wait_recv()
            relay_copy(q, k).start()

    @pl.loop(0, COL_CHUNKS)
    def _(q):
        @pl.loop(0, chips)
        def _(k):
            relay_copy(q, k).wait_recv()

    stores[3].start()

    @pl.loop(0, ROW_CHUNKS)
    def _(r):
        span = pl.ds(pl.multiple_of(r * rc, rc), rc)
        value = z_own[span, :]
        for k in range(1, depth):
            z_copy(k, r).wait_recv()
            value = value + z_recv[k - 1, span, :].astype(F32)
        z_out[span, :] = value.astype(BF16)

    stores[4].start()

    count_mate_copy().wait_send()

    @pl.loop(1, chips)
    def _(k):
        count_chip_copy(k).wait_send()

    @pl.loop(0, COL_CHUNKS)
    def _(q):
        mate_copy(q).wait_send()
        relay_copy(q, 0).wait_send()

        @pl.loop(1, chips)
        def _(k):
            chip_copy(q, k).wait_send()
            spread_copy(q, k).wait_send()
            relay_copy(q, k).wait_send()

    @pl.loop(0, ROW_CHUNKS)
    def _(r):
        for k in range(1, depth):
            z_copy(k, r).wait_send()

    for copy in stores:
        copy.wait()


def place_kernel(owner_smem, *refs):
    arrays, sem = refs[:-1], refs[-1]
    count = len(arrays) // 2
    slots = arrays[3].shape[0]
    copies = [
        pltpu.make_async_copy(arrays[3].at[j], arrays[count + 3].at[owner_smem[j]], sem.at[j])
        for j in range(slots)
    ]
    copies += [
        pltpu.make_async_copy(arrays[i], arrays[count + i], sem.at[slots + i])
        for i in range(count)
        if i != 3
    ]
    for copy in copies:
        copy.start()
    for copy in copies:
        copy.wait()


def place(owner_map, results):
    slots, block, columns = results[3].shape
    hbm = pl.BlockSpec(memory_space=pl.ANY)
    outs = pl.pallas_call(
        place_kernel,
        out_shape=tuple(jax.ShapeDtypeStruct(x.shape, x.dtype) for x in results),
        in_specs=[pl.BlockSpec(memory_space=pltpu.SMEM)] + [hbm] * len(results),
        out_specs=(hbm,) * len(results),
        scratch_shapes=[pltpu.SemaphoreType.DMA((slots + len(results),))],
    )(owner_map, *results)
    return (*outs[:3], outs[3].reshape(slots * block, columns), outs[4])


def per_device(
    hidden_acts, out_grads, token_counts, down_weight, owner_map, master, moment1, moment2
):
    rows, columns = out_grads.shape
    hidden = hidden_acts.shape[1]
    slots = lax.axis_size("dp")
    depth = lax.axis_size("mp")
    chips = slots // 2
    block = hidden // slots
    share = hidden // depth
    cc = columns // COL_CHUNKS
    smem = pl.BlockSpec(memory_space=pltpu.SMEM)
    hbm = pl.BlockSpec(memory_space=pl.ANY)
    vmem = pltpu.VMEM
    dma = pltpu.SemaphoreType.DMA
    pieces = (COL_CHUNKS, chips, block, cc)
    results = pl.pallas_call(
        functools.partial(kernel, chips, depth),
        out_shape=(
            jax.ShapeDtypeStruct(master.shape, F32),
            jax.ShapeDtypeStruct(moment1.shape, F32),
            jax.ShapeDtypeStruct(moment2.shape, BF16),
            jax.ShapeDtypeStruct((slots, block, columns), BF16),
            jax.ShapeDtypeStruct((rows, share), BF16),
        ),
        in_specs=[hbm, hbm, smem, hbm, smem, hbm, hbm, hbm],
        out_specs=(hbm,) * 5,
        scratch_shapes=[
            vmem(hidden_acts.shape, BF16),
            vmem((hidden, rows), BF16),
            vmem((rows, columns), BF16),
            vmem((hidden, columns), BF16),
            vmem(master.shape, F32),
            vmem(moment1.shape, F32),
            vmem(moment2.shape, BF16),
            vmem((hidden, hidden), BF16),
            vmem((COL_CHUNKS, chips, 2, block, cc), BF16),
            vmem(pieces, BF16),
            vmem(pieces, BF16),
            vmem(pieces, BF16),
            vmem((COL_CHUNKS, block, cc), F32),
            vmem((slots, block, columns), BF16),
            vmem((depth - 1, rows, share), BF16),
            vmem((depth - 1, rows, share), BF16),
            vmem((rows, share), F32),
            vmem((rows, share), BF16),
            vmem((8, 128), jnp.int32),
            vmem((8, 128), jnp.int32),
            vmem((8, 128), jnp.int32),
            vmem((chips, 8, 128), jnp.int32),
            dma((5,)),
            dma((ROW_CHUNKS,)),
            dma((5,)),
            dma((COL_CHUNKS,)),
            dma((COL_CHUNKS,)),
            dma((COL_CHUNKS, chips)),
            dma((COL_CHUNKS, chips)),
            dma((COL_CHUNKS, chips)),
            dma((COL_CHUNKS, chips)),
            dma((COL_CHUNKS, chips)),
            dma((COL_CHUNKS, chips)),
            dma((depth - 1, ROW_CHUNKS)),
            dma((depth - 1, ROW_CHUNKS)),
            dma((chips,)),
            dma((chips,)),
        ],
        compiler_params=pltpu.CompilerParams(
            collective_id=0, has_side_effects=True, vmem_limit_bytes=60 * 1024 * 1024
        ),
        cost_estimate=pl.CostEstimate(
            flops=4 * rows * columns * hidden,
            bytes_accessed=2 * (rows * hidden + rows * columns + 2 * hidden * columns),
            transcendentals=0,
        ),
    )(hidden_acts, out_grads, token_counts, down_weight, owner_map, master, moment1, moment2)
    return place(owner_map, results)


def solution(mesh):
    in_specs = (
        P("dp", None),
        P("dp", "mp"),
        P("dp"),
        P(None, "mp"),
        P(),
        P("dp", "mp"),
        P("dp", "mp"),
        P("dp", "mp"),
    )
    out_specs = (P("dp", "mp"), P("dp", "mp"), P("dp", "mp"), P(None, "mp"), P("dp", "mp"))
    return jax.shard_map(
        per_device, mesh=mesh, in_specs=in_specs, out_specs=out_specs, check_vma=False
    )
```

```python
import functools

import jax
import jax.numpy as jnp
from jax import lax
from jax.experimental import pallas as pl
from jax.experimental.pallas import tpu as pltpu
from jax.sharding import PartitionSpec as P

beta_one = 0.9
beta_two = 0.95
learn_rate = 0.0003
epsilon = 1e-08
correct_one = 1.0 - 0.9**50
correct_two = 1.0 - 0.95**50

MESH = pl.DeviceIdType.MESH
F32 = jnp.float32
BF16 = jnp.bfloat16
ROW_CHUNKS = 4
COL_CHUNKS = 4


def kernel(
    chips, depth,
    acts_hbm, grads_hbm, count_smem, weight_hbm, owner_smem, master_hbm, moment1_hbm, moment2_hbm,
    master_out, moment1_out, moment2_out, weights_out, input_out,
    acts, acts_t, grads, weight, master, moment1, moment2,
    pick, part, from_mate, to_chip, from_chip, own_sum,
    gathered, z_half, z_in, z_part, z_full, z_out,
    count_tile, count_mate, count_pair, count_chip,
    load_sem, grads_sem, out_sem,
    mate_send, mate_recv, chip_send, chip_recv,
    spread_send, spread_recv, relay_send, relay_recv,
    half_send, half_recv, full_send, full_recv, count_send, count_recv,
):
    rows, columns = grads.shape
    hidden = acts.shape[1]
    slots = 2 * chips
    block = hidden // slots
    share = hidden // depth
    rc = rows // ROW_CHUNKS
    cc = columns // COL_CHUNKS
    tile = 256

    me = lax.axis_index("dp")
    z = lax.axis_index("mp")
    core = lax.rem(me, 2)
    chip = me // 2
    mate = me + 1 - 2 * core
    mate_id = (mate, z)

    def chip_id(k):
        return (2 * lax.rem(chip + k, chips) + core, z)

    def z_id(k):
        return (me, lax.rem(z + k, depth))

    def grads_copy(r):
        span = pl.ds(pl.multiple_of(r * rc, rc), rc)
        return pltpu.make_async_copy(grads_hbm.at[span], grads.at[span], grads_sem.at[r])

    for r in range(ROW_CHUNKS):
        grads_copy(r).start()
    loads = [
        pltpu.make_async_copy(source, target, load_sem.at[i])
        for i, (source, target) in enumerate(
            [
                (weight_hbm, weight),
                (acts_hbm, acts),
                (master_hbm, master),
                (moment1_hbm, moment1),
                (moment2_hbm, moment2),
            ]
        )
    ]
    for copy in loads:
        copy.start()

    barrier = pltpu.get_barrier_semaphore()
    pl.semaphore_signal(barrier, inc=1, device_id=mate_id, device_id_type=MESH)

    @pl.loop(1, chips)
    def _(k):
        pl.semaphore_signal(barrier, inc=1, device_id=chip_id(k), device_id_type=MESH)

    for k in range(1, depth):
        pl.semaphore_signal(barrier, inc=1, device_id=z_id(k), device_id_type=MESH)
    pl.semaphore_wait(barrier, 1 + (chips - 1) + (depth - 1))

    count = count_smem[0]
    count_tile[...] = jnp.full(count_tile.shape, count, jnp.int32)

    def count_mate_copy():
        return pltpu.make_async_remote_copy(
            count_tile, count_mate, count_send.at[0], count_recv.at[0], mate_id, MESH
        )

    def count_chip_copy(k):
        return pltpu.make_async_remote_copy(
            count_pair, count_chip.at[k], count_send.at[k], count_recv.at[k], chip_id(k), MESH
        )

    count_mate_copy().start()

    def feature(r, target):
        span = pl.ds(pl.multiple_of(r * rc, rc), rc)
        value = lax.dot_general(
            grads[span, :],
            weight[pl.ds(pl.multiple_of(target * share, share), share), :],
            (((1,), (1,)), ((), ())),
            preferred_element_type=F32,
        )
        position = lax.broadcasted_iota(jnp.int32, value.shape, 0) + r * rc
        return span, jnp.where(position < count, value, 0.0)

    def aim(way, c):
        target = depth - 1 - c if way == 0 else c
        taking = z < target if way == 0 else z > target
        hop = z if way == 0 else depth - 1 - z
        neighbour = (me, z + 1 if way == 0 else z - 1)
        return target, taking, hop, neighbour

    def half_copy(way, c, r):
        span = pl.ds(pl.multiple_of(r * rc, rc), rc)
        target, _, _, neighbour = aim(way, c)
        return pltpu.make_async_remote_copy(
            z_half.at[target, span], z_in.at[way, c, span],
            half_send.at[way, c, r], half_recv.at[way, c, r], neighbour, MESH,
        )

    def full_copy(way, r):
        span = pl.ds(pl.multiple_of(r * rc, rc), rc)
        target, _, _, neighbour = aim(way, 0)
        return pltpu.make_async_remote_copy(
            z_part.at[target, span], z_full.at[way, span],
            full_send.at[way, r], full_recv.at[way, r], neighbour, MESH,
        )

    def feature_block(way, c):
        target, taking, hop, _ = aim(way, c)

        @pl.when(taking)
        def _():
            @pl.loop(0, ROW_CHUNKS)
            def _(r):
                if c == 0:

                    @pl.when(z < depth - 1 if way == 0 else z == depth - 1)
                    def _():
                        grads_copy(r).wait()

                span, value = feature(r, target)

                @pl.when(hop == 0)
                def _():
                    z_half[target, span, :] = value.astype(BF16)
                    half_copy(way, c, r).start()

                @pl.when(hop > 0)
                def _():
                    z_part[target, span, :] = value

    def forward(c, step):
        for way in range(2):
            target, taking, hop, _ = aim(way, c)
            r = step - hop

            @pl.when(taking & (hop > 0) & (r >= 0) & (r < ROW_CHUNKS))
            def _():
                span = pl.ds(pl.multiple_of(r * rc, rc), rc)
                if c > 0:
                    half_copy(way, c, r).wait_recv()
                    value = z_part[target, span, :] + z_in[way, c, span, :].astype(F32)
                    z_half[target, span, :] = value.astype(BF16)
                    half_copy(way, c, r).start()
                else:

                    @pl.when(hop == 1)
                    def _():
                        half_copy(way, c, r).wait_recv()
                        z_part[target, span, :] += z_in[way, c, span, :].astype(F32)

                    @pl.when(hop > 1)
                    def _():
                        full_copy(way, r).wait_recv()
                        z_part[target, span, :] += z_full[way, span, :]

                    full_copy(way, r).start()

    last_step = ROW_CHUNKS + depth - 3
    forwards = [(c, step) for c in range(depth - 2) for step in range(1, last_step + 1)]

    def forward_some(count):
        for _ in range(min(count, len(forwards))):
            forward(*forwards.pop(0))

    loads[0].wait()
    feature_block(0, 0)
    feature_block(1, 0)

    count_mate_copy().wait_recv()
    count_pair[...] = count_tile[...] + count_mate[...]

    @pl.loop(1, chips)
    def _(k):
        count_chip_copy(k).start()

    loads[1].wait()

    @pl.loop(0, slots)
    def _(j):
        span = pl.ds(pl.multiple_of(j * block, block), block)
        first = owner_smem[j] * block
        unit = lax.broadcasted_iota(jnp.int32, (block, hidden), 1)
        row = lax.broadcasted_iota(jnp.int32, (block, hidden), 0)
        pick[span, :] = jnp.where(unit == row + first, 1.0, 0.0).astype(BF16)

    @pl.loop(0, hidden // tile)
    def _(i):
        span = pl.ds(pl.multiple_of(i * tile, tile), tile)
        turned = lax.dot_general(
            pick[span, :], acts[...], (((1,), (1,)), ((), ())), preferred_element_type=F32
        )
        position = lax.broadcasted_iota(jnp.int32, turned.shape, 1)
        acts_t[span, :] = jnp.where(position < count, turned, 0.0).astype(BF16)

    def mate_copy(q):
        return pltpu.make_async_remote_copy(
            part.at[q, :, 1 - core], from_mate.at[q], mate_send.at[q], mate_recv.at[q],
            mate_id, MESH,
        )

    def chip_copy(q, k):
        return pltpu.make_async_remote_copy(
            to_chip.at[q, k], from_chip.at[q, k], chip_send.at[q, k], chip_recv.at[q, k],
            chip_id(k), MESH,
        )

    pairs = tile // (2 * block)

    def partial_chunk(q):
        across = pl.ds(pl.multiple_of(q * cc, cc), cc)

        @pl.loop(0, hidden // tile)
        def _(i):
            span = pl.ds(pl.multiple_of(i * tile, tile), tile)
            value = jnp.dot(acts_t[span, :], grads[:, across], preferred_element_type=F32)
            part[q, pl.ds(i * pairs, pairs)] = value.astype(BF16).reshape(pairs, 2, block, cc)

        mate_copy(q).start()

    def pair_chunk(q):
        mate_copy(q).wait_recv()

        @pl.loop(1, chips)
        def _(k):
            there = lax.rem(chip + k, chips)
            both = part[q, there, core].astype(F32) + from_mate[q, there].astype(F32)
            to_chip[q, k] = both.astype(BF16)
            chip_copy(q, k).start()

        own_sum[q] = part[q, chip, core].astype(F32) + from_mate[q, chip].astype(F32)

    forward_some(1)
    for q in range(COL_CHUNKS):
        partial_chunk(q)
        if q > 0:
            pair_chunk(q - 1)
        if q == COL_CHUNKS // 2:
            forward_some(1)
    pair_chunk(COL_CHUNKS - 1)

    for c in range(1, depth - 1):
        feature_block(0, c)
        feature_block(1, c)
        if c == 1:
            forward_some(1)

    @pl.loop(0, ROW_CHUNKS)
    def _(r):
        span, value = feature(r, z)
        z_part[z, span, :] = value

    @pl.loop(1, chips)
    def _(k):
        count_chip_copy(k).wait_recv()

    total = lax.fori_loop(1, chips, lambda k, t: t + count_chip[k], count_pair[...])
    total = total[0:1, 0:1].astype(F32)
    for copy in loads[2:]:
        copy.wait()

    def spread_copy(q, k):
        across = pl.ds(pl.multiple_of(q * cc, cc), cc)
        return pltpu.make_async_remote_copy(
            gathered.at[me, :, across], gathered.at[me, :, across],
            spread_send.at[q, k], spread_recv.at[q, k], chip_id(k), MESH,
        )

    def relay_copy(q, k):
        slot = 2 * lax.rem(chip + chips - k, chips) + core
        across = pl.ds(pl.multiple_of(q * cc, cc), cc)
        return pltpu.make_async_remote_copy(
            gathered.at[slot, :, across], gathered.at[slot, :, across],
            relay_send.at[q, k], relay_recv.at[q, k], mate_id, MESH,
        )

    def update_chunk(q):
        across = pl.ds(pl.multiple_of(q * cc, cc), cc)

        @pl.loop(1, chips)
        def _(k):
            chip_copy(q, k).wait_recv()
            own_sum[q] = own_sum[q] + from_chip[q, k].astype(F32)

        grad = own_sum[q] / total
        moment1_new = beta_one * moment1[:, across] + (1.0 - beta_one) * grad
        second = beta_two * moment2[:, across].astype(F32) + (1.0 - beta_two) * grad * grad
        moment1[:, across] = moment1_new
        moment2[:, across] = second.astype(BF16)
        master_new = master[:, across] - learn_rate * (moment1_new / correct_one) / (
            jnp.sqrt(second / correct_two) + epsilon
        )
        master[:, across] = master_new
        gathered[me, :, across] = master_new.astype(BF16)

        @pl.loop(1, chips)
        def _(k):
            spread_copy(q, k).start()

        relay_copy(q, 0).start()

    for q in range(COL_CHUNKS):
        update_chunk(q)
        if q > 0:
            forward_some(1)

    stores = [
        pltpu.make_async_copy(source, target, out_sem.at[i])
        for i, (source, target) in enumerate(
            [
                (master, master_out),
                (moment1, moment1_out),
                (moment2, moment2_out),
                (gathered, weights_out),
                (z_out, input_out),
            ]
        )
    ]
    for copy in stores[:3]:
        copy.start()

    forward_some(len(forwards))

    @pl.loop(0, COL_CHUNKS)
    def _(q):
        @pl.loop(1, chips)
        def _(k):
            spread_copy(q, k).wait_recv()
            relay_copy(q, k).start()

    @pl.loop(0, COL_CHUNKS)
    def _(q):
        @pl.loop(0, chips)
        def _(k):
            relay_copy(q, k).wait_recv()

    stores[3].start()

    @pl.loop(0, ROW_CHUNKS)
    def _(r):
        span = pl.ds(pl.multiple_of(r * rc, rc), rc)
        for way in range(2):
            hop = z if way == 0 else depth - 1 - z
            c = depth - 1 - hop
            wide = (hop == depth - 1) & (depth > 2)

            @pl.when((hop > 0) & wide)
            def _():
                full_copy(way, r).wait_recv()
                z_part[z, span, :] += z_full[way, span, :]

            @pl.when((hop > 0) & jnp.logical_not(wide))
            def _():
                half_copy(way, c, r).wait_recv()
                z_part[z, span, :] += z_in[way, c, span, :].astype(F32)

        z_out[span, :] = z_part[z, span, :].astype(BF16)

    stores[4].start()

    count_mate_copy().wait_send()

    @pl.loop(1, chips)
    def _(k):
        count_chip_copy(k).wait_send()

    @pl.loop(0, COL_CHUNKS)
    def _(q):
        mate_copy(q).wait_send()
        relay_copy(q, 0).wait_send()

        @pl.loop(1, chips)
        def _(k):
            chip_copy(q, k).wait_send()
            spread_copy(q, k).wait_send()
            relay_copy(q, k).wait_send()

    @pl.loop(0, ROW_CHUNKS)
    def _(r):
        for way in range(2):
            for c in range(depth - 1):
                _, taking, hop, _ = aim(way, c)

                @pl.when(taking & (hop == 0) if c == 0 else taking)
                def _():
                    half_copy(way, c, r).wait_send()

            _, taking, hop, _ = aim(way, 0)

            @pl.when(taking & (hop > 0))
            def _():
                full_copy(way, r).wait_send()

    for copy in stores:
        copy.wait()


def place_kernel(owner_smem, *refs):
    count = len(refs) // 3
    sources, targets, held = refs[:count], refs[count : 2 * count], refs[2 * count : 3 * count]
    in_sem, out_sem = refs[3 * count :]
    slots = held[3].shape[0]
    moves = [
        (sources[3].at[j], held[3].at[j], targets[3].at[owner_smem[j]]) for j in range(slots)
    ]
    moves += [(sources[i], held[i], targets[i]) for i in range(count) if i != 3]
    fills = [pltpu.make_async_copy(m[0], m[1], in_sem.at[i]) for i, m in enumerate(moves)]
    drains = [pltpu.make_async_copy(m[1], m[2], out_sem.at[i]) for i, m in enumerate(moves)]
    for fill in fills:
        fill.start()
    for fill, drain in zip(fills, drains):
        fill.wait()
        drain.start()
    for drain in drains:
        drain.wait()


def place(owner_map, results):
    slots, block, columns = results[3].shape
    hbm = pl.BlockSpec(memory_space=pl.ANY)
    moves = slots + len(results) - 1
    outs = pl.pallas_call(
        place_kernel,
        out_shape=tuple(jax.ShapeDtypeStruct(x.shape, x.dtype) for x in results),
        in_specs=[pl.BlockSpec(memory_space=pltpu.SMEM)] + [hbm] * len(results),
        out_specs=(hbm,) * len(results),
        scratch_shapes=[pltpu.VMEM(x.shape, x.dtype) for x in results]
        + [pltpu.SemaphoreType.DMA((moves,)), pltpu.SemaphoreType.DMA((moves,))],
        compiler_params=pltpu.CompilerParams(vmem_limit_bytes=60 * 1024 * 1024),
    )(owner_map, *results)
    return (*outs[:3], outs[3].reshape(slots * block, columns), outs[4])


def per_device(
    hidden_acts, out_grads, token_counts, down_weight, owner_map, master, moment1, moment2
):
    rows, columns = out_grads.shape
    hidden = hidden_acts.shape[1]
    slots = lax.axis_size("dp")
    depth = lax.axis_size("mp")
    chips = slots // 2
    block = hidden // slots
    share = hidden // depth
    cc = columns // COL_CHUNKS
    smem = pl.BlockSpec(memory_space=pltpu.SMEM)
    hbm = pl.BlockSpec(memory_space=pl.ANY)
    vmem = pltpu.VMEM
    dma = pltpu.SemaphoreType.DMA
    pieces = (COL_CHUNKS, chips, block, cc)
    results = pl.pallas_call(
        functools.partial(kernel, chips, depth),
        out_shape=(
            jax.ShapeDtypeStruct(master.shape, F32),
            jax.ShapeDtypeStruct(moment1.shape, F32),
            jax.ShapeDtypeStruct(moment2.shape, BF16),
            jax.ShapeDtypeStruct((slots, block, columns), BF16),
            jax.ShapeDtypeStruct((rows, share), BF16),
        ),
        in_specs=[hbm, hbm, smem, hbm, smem, hbm, hbm, hbm],
        out_specs=(hbm,) * 5,
        scratch_shapes=[
            vmem(hidden_acts.shape, BF16),
            vmem((hidden, rows), BF16),
            vmem((rows, columns), BF16),
            vmem((hidden, columns), BF16),
            vmem(master.shape, F32),
            vmem(moment1.shape, F32),
            vmem(moment2.shape, BF16),
            vmem((hidden, hidden), BF16),
            vmem((COL_CHUNKS, chips, 2, block, cc), BF16),
            vmem(pieces, BF16),
            vmem(pieces, BF16),
            vmem(pieces, BF16),
            vmem((COL_CHUNKS, block, cc), F32),
            vmem((slots, block, columns), BF16),
            vmem((depth, rows, share), BF16),
            vmem((2, depth - 1, rows, share), BF16),
            vmem((depth, rows, share), F32),
            vmem((2, rows, share), F32),
            vmem((rows, share), BF16),
            vmem((8, 128), jnp.int32),
            vmem((8, 128), jnp.int32),
            vmem((8, 128), jnp.int32),
            vmem((chips, 8, 128), jnp.int32),
            dma((5,)),
            dma((ROW_CHUNKS,)),
            dma((5,)),
            dma((COL_CHUNKS,)),
            dma((COL_CHUNKS,)),
            dma((COL_CHUNKS, chips)),
            dma((COL_CHUNKS, chips)),
            dma((COL_CHUNKS, chips)),
            dma((COL_CHUNKS, chips)),
            dma((COL_CHUNKS, chips)),
            dma((COL_CHUNKS, chips)),
            dma((2, depth - 1, ROW_CHUNKS)),
            dma((2, depth - 1, ROW_CHUNKS)),
            dma((2, ROW_CHUNKS)),
            dma((2, ROW_CHUNKS)),
            dma((chips,)),
            dma((chips,)),
        ],
        compiler_params=pltpu.CompilerParams(
            collective_id=0, has_side_effects=True, vmem_limit_bytes=60 * 1024 * 1024
        ),
        cost_estimate=pl.CostEstimate(
            flops=4 * rows * columns * hidden,
            bytes_accessed=2 * (rows * hidden + rows * columns + 2 * hidden * columns),
            transcendentals=0,
        ),
    )(hidden_acts, out_grads, token_counts, down_weight, owner_map, master, moment1, moment2)
    return place(owner_map, results)


def solution(mesh):
    in_specs = (
        P("dp", None),
        P("dp", "mp"),
        P("dp"),
        P(None, "mp"),
        P(),
        P("dp", "mp"),
        P("dp", "mp"),
        P("dp", "mp"),
    )
    out_specs = (P("dp", "mp"), P("dp", "mp"), P("dp", "mp"), P(None, "mp"), P("dp", "mp"))
    return jax.shard_map(
        per_device, mesh=mesh, in_specs=in_specs, out_specs=out_specs, check_vma=False
    )
```
